32 devices in a mesh: parts: 2 (over x), tensor: 16 (over z, y, core).
Axes of the slice: x: 2, y: 2, z: 4, core: 2. Of those that a mesh axis runs over, the one named last changes fastest.
Arguments:
- tokens: bfloat16 [512, 8192], P(('parts', 'tensor')), parts along dimension 0, may hold values from -6 to 6
- out_grad: bfloat16 [512, 8192], P(('parts', 'tensor')), parts along dimension 0, may hold values from -6 to 6
- gate_weight: bfloat16 [8192, 20480], P(None, 'tensor'), may hold values from -0.0625 to 0.0625
- down_weight: bfloat16 [20480, 8192], P('tensor'), may hold values from -0.0390625 to 0.0390625
- proj_in: bfloat16 [8192, 64], replicated, may hold values from -0.0625 to 0.0625
- proj_out: bfloat16 [20480, 64], P('tensor'), may hold values from -0.0390625 to 0.0390625
- lengths: int32 [8], P('parts'), parts along dimension 0, may hold values from 1 to 128, 256 in all
- query_features: float32 [1024, 4096], P(None, 'tensor'), may hold values from -0.1 to 0.1
Outputs:
- train_features: float32 [8, 4096], P('parts', 'tensor'), parts along dimension 0
- scores: float32 [8, 1024], P('parts'), parts along dimension 0
The draws below stay inside these ranges and needn't reach their ends.
There are 2 independent parts, one for each index of `parts`. The reference program is written for one: setup_inputs(seed, part) draws one part's arguments, and reference() takes and returns one part's arrays. A program takes and returns all parts, laid end to end along the dimension named above; an argument that names none is the same for every part. Nothing has to cross between parts.
Inputs may be any that keep to these rules, and one draw needn't show every extreme that they name: The lengths sum to 256, and the largest is exactly 128.
All inputs are finite; a program needn't handle non-finite values.
Results may differ from the reference program's by a relative error of at most 0.0031.
Values may be sent and summed in bfloat16 or wider, within the bound.
A program may use at most 192 MiB of HBM per device.

```python
import math
import jax
import jax.numpy as jnp
import numpy as np
from jax import lax

D = 8192
FF = 20480
RANK = 64
EXAMPLES = 4
QUERIES = 1024
TOKENS = 256


def steps_of(rng, dims, split, smallest, high):
    def one(position, shards_of):
        draws = jax.random.uniform(jax.random.fold_in(jax.random.fold_in(rng, 6), position), (shards_of,), jnp.float32, smallest / len(split), high / len(split))
        return jnp.repeat(jnp.exp(draws), dims[position] // shards_of).reshape((-1,) + (1,) * (len(dims) - position - 1))

    gain = one(*split[0])
    for cut in split[1:]:
        gain = gain * one(*cut)
    return gain


def profile(number_of, total, most, slope):
    loads = [(1 << 20) // math.isqrt(grade ** slope) + 1 for grade in range(2, number_of + 1)]
    rest, counts = total - most - (number_of - 1), [1] * (number_of - 1)
    while rest > 0:
        candidates = [i for i in range(number_of - 1) if counts[i] < most]
        whole, left = sum([loads[i] for i in candidates]), rest
        for i in candidates:
            more = min(most - counts[i], max(1, left * loads[i] // whole), rest)
            counts[i] = counts[i] + more
            rest = rest - more
    return np.array([most] + counts)


def ragged(own_key, count, total, most, skew):
    if count == 2:
        one = jax.random.randint(own_key, (), max(1, total - most), min(most, total - 1) + 1)
        return jnp.stack([one, total - one])
    sizes = jnp.asarray(profile(count, total, most, skew), jnp.int32)
    pairs = (count - 1) // 2
    source_of, receiver = sizes[1:1 + 2 * pairs:2], sizes[2:2 + 2 * pairs:2]
    margin = jnp.minimum(source_of - 1, most - receiver)
    passed = jax.random.randint(jax.random.fold_in(own_key, 1), (pairs,), 0, 1 << 20) % (margin + 1)
    sizes = sizes.at[1:1 + 2 * pairs:2].set(source_of - passed).at[2:2 + 2 * pairs:2].set(receiver + passed)
    return sizes[jax.random.permutation(jax.random.fold_in(own_key, 2), count)]


def gaussian(stream_key, extent, scale, reach, pieces=(), held_as=jnp.bfloat16):
    gain = steps_of(stream_key, extent, pieces, -0.22, 0.18) if pieces else 1.0
    values = jax.random.normal(stream_key, extent, jnp.float32) * scale * gain
    return jnp.minimum(jnp.maximum(values, -reach), reach).astype(held_as)


def setup_inputs(seed: int = 0, part: int = 0) -> dict:
    seeds = jax.random.split(jax.random.key(seed), 9)
    part_splits = jax.random.split(jax.random.fold_in(seeds[8], part), 9)
    return {
        "tokens": gaussian(part_splits[0], (TOKENS, D), 1.0, 6.0, ((0, 16),)),
        "out_grad": gaussian(part_splits[1], (TOKENS, D), 1.0, 6.0, ((0, 16),)),
        "gate_weight": gaussian(seeds[2], (D, FF), D ** -0.5, 0.0625, ((1, 16),)),
        "down_weight": gaussian(seeds[3], (FF, D), FF ** -0.5, 0.0390625, ((0, 16),)),
        "proj_in": gaussian(seeds[4], (D, RANK), D ** -0.5, 0.0625),
        "proj_out": gaussian(seeds[5], (FF, RANK), FF ** -0.5, 0.0390625, ((0, 16),)),
        "lengths": ragged(part_splits[6], EXAMPLES, TOKENS, TOKENS // 2, 2).astype(jnp.int32),
        "query_features": gaussian(seeds[7], (QUERIES, RANK * RANK), 0.015625, 0.1, ((1, 16),), jnp.float32),
    }


def kron_features(member, proj_x, proj_g):
    rows = proj_x.shape[0]
    width = proj_x.shape[1]
    count = member.shape[1]
    weighted = (member[:, :, None] * proj_x[:, None, :]).reshape(rows, count * width)
    feats = lax.dot_general(weighted, proj_g, (((0,), (0,)), ((), ())), precision=lax.Precision.HIGHEST)
    return feats.reshape(count, width * proj_g.shape[1])


def membership(lengths, rows):
    ends = jnp.cumsum(lengths).astype(jnp.int32)
    starts = (ends - lengths).astype(jnp.int32)
    place = jnp.arange(rows, dtype=jnp.int32)[:, None]
    inside = (place >= starts[None, :]) & (place < ends[None, :])
    return inside.astype(jnp.float32)


def reference(tokens, out_grad, gate_weight, down_weight, proj_in, proj_out, lengths, query_features):
    gate = jnp.dot(tokens, gate_weight, preferred_element_type=jnp.float32)
    grad_hidden = lax.dot_general(out_grad, down_weight, (((1,), (1,)), ((), ())), preferred_element_type=jnp.float32)
    grad_up = (grad_hidden * jax.nn.silu(gate)).astype(jnp.bfloat16)
    proj_x = jnp.dot(tokens, proj_in, preferred_element_type=jnp.float32)
    proj_g = jnp.dot(grad_up, proj_out, preferred_element_type=jnp.float32)
    member = membership(lengths, tokens.shape[0])
    feats = kron_features(member, proj_x, proj_g)
    scores = lax.dot_general(feats, query_features, (((1,), (1,)), ((), ())), precision=lax.Precision.HIGHEST)
    return feats, scores
```

```python
import functools

import jax
import jax.numpy as jnp
from jax import lax
from jax.experimental import pallas as pl
from jax.experimental.pallas import tpu as pltpu
from jax.sharding import PartitionSpec as P

F32 = jnp.float32
BF16 = jnp.bfloat16
CHUNK = 1024
LAG = 1
TILE = 256


def nt(a, b, precision=None):
    return lax.dot_general(
        a, b, (((1,), (1,)), ((), ())), precision=precision, preferred_element_type=F32
    )


def kernel(
    n, tok, dy, wg, wd, pin, pout, lens, q, feats_ref, scores_ref,
    buf, wgv, wdv, gate, hidden, pinv, poutv, qv, px, wt, fpart, frecv, spart, srecv, zrecv,
    own_sem, wg_sem, wd_sem, misc_sem, up_sem, dn_sem, ys_sem, cs_sem, zr_sem, yr_sem, cr_sem,
    fs_sem, fr_sem, ss_sem, sr_sem, zs_sem, zrr_sem,
):
    me = lax.axis_index("tensor")
    rows = tok.shape[0]
    lines = n // 4
    c = lax.rem(me, 2)
    y = lax.rem(me // 2, 2)
    z = me // 4
    jobs = buf.shape[0]
    half = jobs // 2
    total = buf.shape[1]
    examples = lens.shape[0]

    def index(zz, yy, cc):
        return (zz * 2 + yy) * 2 + cc

    def row(cc, yy, zz):
        return pl.multiple_of(((cc * 2 + yy) * lines + zz) * rows, rows)

    def own_copy(src, k, j):
        return pltpu.make_async_copy(
            src.at[:, pl.ds(pl.multiple_of(k * CHUNK, CHUNK), CHUNK)],
            buf.at[j, pl.ds(row(c, y, z), rows)], own_sem.at[j])

    def wg_copy(k):
        return pltpu.make_async_copy(
            wg.at[pl.ds(pl.multiple_of(k * CHUNK, CHUNK), CHUNK)], wgv.at[k], wg_sem.at[k])

    def wd_copy(k):
        return pltpu.make_async_copy(
            wd.at[:, pl.ds(pl.multiple_of(k * CHUNK, CHUNK), CHUNK)], wdv.at[k], wd_sem.at[k])

    small = [
        pltpu.make_async_copy(pin, pinv, misc_sem.at[0]),
        pltpu.make_async_copy(pout, poutv, misc_sem.at[1]),
        pltpu.make_async_copy(q, qv, misc_sem.at[2]),
    ]

    @pl.loop(0, half)
    def _(k):
        own_copy(tok, k, k).start()
        own_copy(dy, k, k + half).start()

    small[0].start()

    @pl.loop(0, half)
    def _(k):
        wg_copy(k).start()

    @pl.loop(0, half)
    def _(k):
        wd_copy(k).start()

    small[1].start()
    small[2].start()

    barrier = pltpu.get_barrier_semaphore()
    for i in range(1, n):
        pl.semaphore_signal(barrier, inc=1, device_id={"tensor": lax.rem(me + i, n)})
    pl.semaphore_wait(barrier, n - 1)

    gate[...] = jnp.zeros_like(gate)
    hidden[...] = jnp.zeros_like(hidden)
    px[...] = jnp.zeros_like(px)

    def block(j, start, size, send, recv, device):
        part = buf.at[j, pl.ds(start, size)]
        return pltpu.make_async_remote_copy(
            src_ref=part, dst_ref=part, send_sem=send, recv_sem=recv,
            device_id={"tensor": device})

    def up(j, o):
        return block(j, row(c, y, o), rows, up_sem.at[j], zr_sem.at[j, o], index(z + 1, y, c))

    def down(j, o):
        return block(j, row(c, y, o), rows, dn_sem.at[j], zr_sem.at[j, o], index(z - 1, y, c))

    def across(j, o):
        return block(j, row(c, y, o), rows, ys_sem.at[j], yr_sem.at[j], index(z, 1 - y, c))

    def twin(j, which, yy):
        return block(
            j, row(c, yy, 0), rows * lines, cs_sem.at[j, which], cr_sem.at[j, which],
            index(z, y, 1 - c))

    def arrived(j, start, size, sem):
        part = buf.at[j, pl.ds(start, size)]
        pltpu.make_async_copy(part, part, sem).wait()

    def inside(j):
        return jnp.logical_and(j >= 0, j < jobs)

    def step(s, carry):
        @pl.when(s < jobs)
        def _():
            arrived(s, row(c, y, z), rows, own_sem.at[s])

            @pl.when(z < lines - 1)
            def _():
                up(s, z).start()

            @pl.when(z > 0)
            def _():
                down(s, z).start()

            across(s, z).start()

        for h in range(1, lines):
            j = s - h * LAG

            @pl.when(jnp.logical_and(inside(j), z >= h))
            def _():
                o = z - h
                arrived(j, row(c, y, o), rows, zr_sem.at[j, o])

                @pl.when(z < lines - 1)
                def _():
                    up(j, o).start()

                across(j, o).start()

            @pl.when(jnp.logical_and(inside(j), z + h < lines))
            def _():
                o = z + h
                arrived(j, row(c, y, o), rows, zr_sem.at[j, o])

                @pl.when(z > 0)
                def _():
                    down(j, o).start()

                across(j, o).start()

        j1 = s - (lines - 1) * LAG

        @pl.when(inside(j1))
        def _():
            twin(j1, 0, y).start()

        j2 = s - lines * LAG

        @pl.when(inside(j2))
        def _():
            arrived(j2, row(c, 1 - y, 0), rows * lines, yr_sem.at[j2])
            twin(j2, 1, 1 - y).start()

        j3 = s - (lines + 1) * LAG

        @pl.when(inside(j3))
        def _():
            arrived(j3, row(1 - c, y, 0), rows * lines, cr_sem.at[j3, 0])
            arrived(j3, row(1 - c, 1 - y, 0), rows * lines, cr_sem.at[j3, 1])

        @pl.when(jnp.logical_and(j3 >= 0, j3 < half))
        def _():
            wg_copy(j3).wait()

            @pl.when(j3 == 0)
            def _():
                small[0].wait()

            @pl.loop(0, gate.shape[0])
            def _(t):
                gate[t] += jnp.dot(
                    buf[j3], wgv[j3, :, pl.ds(pl.multiple_of(t * gate.shape[2], 128), gate.shape[2])],
                    preferred_element_type=F32)

            px[...] += jnp.dot(
                buf[j3], pinv[pl.ds(pl.multiple_of(j3 * CHUNK, CHUNK), CHUNK)],
                preferred_element_type=F32)

        @pl.when(jnp.logical_and(j3 >= half, j3 < jobs))
        def _():
            k = j3 - half
            wd_copy(k).wait()

            @pl.loop(0, hidden.shape[0])
            def _(t):
                hidden[t] += nt(
                    buf[j3], wdv[k, pl.ds(pl.multiple_of(t * gate.shape[2], 128), hidden.shape[2])])

            @pl.when(k == 0)
            def _():
                @pl.loop(0, gate.shape[0])
                def _(t):
                    g = gate[t]
                    gate[t] = g / (1.0 + jnp.exp(-g))

                weighted()

        return carry

    width = px.shape[1]
    each = fpart.shape[0] // n
    per = each // examples

    def weighted():
        r = lax.broadcasted_iota(jnp.int32, (fpart.shape[0], width), 0)
        col = lax.broadcasted_iota(jnp.int32, (fpart.shape[0], width), 1)
        pick = jnp.where(r // examples == col, 1.0, 0.0).astype(F32)
        spread = nt(pick, px[...], lax.Precision.HIGHEST)
        e = lax.rem(lax.broadcasted_iota(jnp.int32, spread.shape, 0), examples)
        at = lax.broadcasted_iota(jnp.int32, spread.shape, 1)
        piece = at // rows
        oz = lax.rem(piece, lines)
        oy = lax.rem(piece // lines, 2)
        oc = piece // (2 * lines)
        token = index(oz, oy, oc) * rows + lax.rem(at, rows)
        begin = jnp.int32(0)
        mask = jnp.zeros(spread.shape, F32)
        for i in range(examples):
            end = begin + lens[i]
            mine = (e == i) & (token >= begin) & (token < end)
            mask = mask + jnp.where(mine, 1.0, 0.0)
            begin = end
        wt[...] = spread * mask

    lax.fori_loop(0, jobs + (lines + 1) * LAG, step, 0)

    small[1].wait()
    part_g = jnp.zeros((total, width), F32)
    for t in range(gate.shape[0]):
        grad_up = (hidden[t] * gate[t]).astype(BF16)
        part_g += jnp.dot(
            grad_up, poutv[t * gate.shape[2]:(t + 1) * gate.shape[2]], preferred_element_type=F32)
    fpart[...] = jnp.dot(
        wt[...], part_g, precision=lax.Precision.HIGHEST, preferred_element_type=F32)

    def deal(i):
        d = lax.rem(me + i, n)
        return pltpu.make_async_remote_copy(
            src_ref=fpart.at[pl.ds(pl.multiple_of(d * each, each), each)],
            dst_ref=frecv.at[i - 1], send_sem=fs_sem.at[i - 1], recv_sem=fr_sem.at[i - 1],
            device_id={"tensor": d})

    for i in range(1, n):
        deal(i).start()
    small[2].wait()
    mine = fpart[pl.ds(pl.multiple_of(me * each, each), each)]
    for i in range(1, n):
        deal(i).wait_recv()
    for i in range(1, n):
        mine = mine + frecv[i - 1]
    for i in range(per):
        feats_ref[:, i * width:(i + 1) * width] = mine[i * examples:(i + 1) * examples]
    spart[0] = nt(feats_ref[...], qv[...], lax.Precision.HIGHEST)

    def plane(p):
        yy, cc = lax.rem(y + p // 2, 2), lax.rem(c + p % 2, 2)
        return pltpu.make_async_remote_copy(
            src_ref=spart.at[0], dst_ref=srecv.at[p - 1], send_sem=ss_sem.at[p - 1],
            recv_sem=sr_sem.at[p - 1], device_id={"tensor": index(z, yy, cc)})

    def along(p):
        return pltpu.make_async_remote_copy(
            src_ref=spart.at[1], dst_ref=zrecv.at[p - 1], send_sem=zs_sem.at[p - 1],
            recv_sem=zrr_sem.at[p - 1], device_id={"tensor": index(lax.rem(z + p, lines), y, c)})

    for p in range(1, 4):
        plane(p).start()
    acc = spart[0]
    for p in range(1, 4):
        plane(p).wait_recv()
        acc = acc + srecv[p - 1]
    spart[1] = acc
    for p in range(1, lines):
        along(p).start()

    @pl.loop(0, jobs)
    def _(j):
        for zz in range(lines):
            @pl.when(jnp.logical_and(z == zz, zz < lines - 1))
            def _():
                arrived(j, 0, rows * (zz + 1), up_sem.at[j])

            @pl.when(jnp.logical_and(z == zz, zz > 0))
            def _():
                arrived(j, 0, rows * (lines - zz), dn_sem.at[j])

        arrived(j, 0, rows * lines, ys_sem.at[j])
        arrived(j, 0, rows * lines, cs_sem.at[j, 0])
        arrived(j, 0, rows * lines, cs_sem.at[j, 1])

    for i in range(1, n):
        deal(i).wait_send()
    for p in range(1, 4):
        plane(p).wait_send()
    for p in range(1, lines):
        along(p).wait_recv()
        acc = acc + zrecv[p - 1]
    for p in range(1, lines):
        along(p).wait_send()
    scores_ref[...] = acc


def on_device(n, tokens, out_grad, gate_weight, down_weight, proj_in, proj_out, lengths, queries):
    rows, depth = tokens.shape
    hidden = gate_weight.shape[1]
    width = proj_in.shape[1]
    count, columns = queries.shape
    examples = lengths.shape[0]
    total = rows * n
    half = depth // CHUNK
    jobs = 2 * half
    tile = TILE if hidden % TILE == 0 else 128
    tiles = hidden // tile
    lines = n // 4
    dma = pltpu.SemaphoreType.DMA
    anywhere = pl.BlockSpec(memory_space=pl.ANY)
    vmem = pl.BlockSpec(memory_space=pltpu.VMEM)
    smem = pl.BlockSpec(memory_space=pltpu.SMEM)
    feat_rows = examples * width
    return pl.pallas_call(
        functools.partial(kernel, n),
        out_shape=(
            jax.ShapeDtypeStruct((examples, columns), F32),
            jax.ShapeDtypeStruct((examples, count), F32),
        ),
        in_specs=[anywhere] * 6 + [smem, anywhere],
        out_specs=(vmem, vmem),
        scratch_shapes=[
            pltpu.VMEM((jobs, total, CHUNK), BF16),
            pltpu.VMEM((half, CHUNK, hidden), BF16),
            pltpu.VMEM((half, hidden, CHUNK), BF16),
            pltpu.VMEM((tiles, total, tile), F32),
            pltpu.VMEM((tiles, total, tile), F32),
            pltpu.VMEM((depth, width), BF16),
            pltpu.VMEM((hidden, width), BF16),
            pltpu.VMEM((count, columns), F32),
            pltpu.VMEM((total, width), F32),
            pltpu.VMEM((feat_rows, total), F32),
            pltpu.VMEM((feat_rows, width), F32),
            pltpu.VMEM((n - 1, feat_rows // n, width), F32),
            pltpu.VMEM((2, examples, count), F32),
            pltpu.VMEM((3, examples, count), F32),
            pltpu.VMEM((lines - 1, examples, count), F32),
            dma((jobs,)), dma((half,)), dma((half,)), dma((3,)),
            dma((jobs,)), dma((jobs,)), dma((jobs,)), dma((jobs, 2)),
            dma((jobs, lines)), dma((jobs,)), dma((jobs, 2)),
            dma((n - 1,)), dma((n - 1,)), dma((3,)), dma((3,)),
            dma((lines - 1,)), dma((lines - 1,)),
        ],
        compiler_params=pltpu.CompilerParams(
            collective_id=0, has_side_effects=True, vmem_limit_bytes=62 * 1024 * 1024
        ),
    )(tokens, out_grad, gate_weight, down_weight, proj_in, proj_out, lengths, queries)


def solution(mesh):
    placed = (
        P(("parts", "tensor"), None),
        P(("parts", "tensor"), None),
        P(None, "tensor"),
        P("tensor", None),
        P(),
        P("tensor", None),
        P("parts"),
        P(None, "tensor"),
    )
    return jax.shard_map(
        functools.partial(on_device, mesh.shape["tensor"]),
        mesh=mesh,
        in_specs=placed,
        out_specs=(P("parts", "tensor"), P("parts", None)),
        check_vma=False,
    )
```

```python
import functools

import jax
import jax.numpy as jnp
from jax import lax
from jax.experimental import pallas as pl
from jax.experimental.pallas import tpu as pltpu
from jax.sharding import PartitionSpec as P

F32 = jnp.float32
BF16 = jnp.bfloat16
CHUNK = 1024
HOP, SIDE, TWIN = 2, 2, 1
TILE = 256


def nt(a, b, precision=None):
    return lax.dot_general(
        a, b, (((1,), (1,)), ((), ())), precision=precision, preferred_element_type=F32
    )


def kernel(
    n, tok, dy, wg, wd, pin, pout, lens, q, feats_ref, scores_ref,
    buf, wgv, wdv, gate, hidden, pinv, poutv, qv, px, wt, fpart, frecv, spart, srecv, zrecv,
    own_sem, wg_sem, wd_sem, misc_sem, up_sem, dn_sem, ys_sem, cs_sem, zr_sem, yr_sem, cr_sem,
    fs_sem, fr_sem, ss_sem, sr_sem, zs_sem, zrr_sem,
):
    me = lax.axis_index("tensor")
    rows = tok.shape[0]
    lines = n // 4
    c = lax.rem(me, 2)
    y = lax.rem(me // 2, 2)
    z = me // 4
    jobs = buf.shape[0]
    half = jobs // 2
    total = buf.shape[1]
    examples = lens.shape[0]

    def index(zz, yy, cc):
        return (zz * 2 + yy) * 2 + cc

    def row(cc, yy, zz):
        return pl.multiple_of(((cc * 2 + yy) * lines + zz) * rows, rows)

    def own_copy(src, k, j):
        return pltpu.make_async_copy(
            src.at[:, pl.ds(pl.multiple_of(k * CHUNK, CHUNK), CHUNK)],
            buf.at[j, pl.ds(row(c, y, z), rows)], own_sem.at[j])

    def wg_copy(k):
        return pltpu.make_async_copy(
            wg.at[pl.ds(pl.multiple_of(k * CHUNK, CHUNK), CHUNK)], wgv.at[k], wg_sem.at[k])

    def wd_copy(k):
        return pltpu.make_async_copy(
            wd.at[:, pl.ds(pl.multiple_of(k * CHUNK, CHUNK), CHUNK)], wdv.at[k], wd_sem.at[k])

    small = [
        pltpu.make_async_copy(pin, pinv, misc_sem.at[0]),
        pltpu.make_async_copy(pout, poutv, misc_sem.at[1]),
        pltpu.make_async_copy(q, qv, misc_sem.at[2]),
    ]

    @pl.loop(0, half)
    def _(k):
        own_copy(tok, k, k).start()
        own_copy(dy, k, k + half).start()

    small[0].start()

    @pl.loop(0, half)
    def _(k):
        wg_copy(k).start()

    @pl.loop(0, half)
    def _(k):
        wd_copy(k).start()

    small[1].start()
    small[2].start()

    barrier = pltpu.get_barrier_semaphore()
    for i in range(1, n):
        pl.semaphore_signal(barrier, inc=1, device_id={"tensor": lax.rem(me + i, n)})
    pl.semaphore_wait(barrier, n - 1)

    gate[...] = jnp.zeros_like(gate)
    hidden[...] = jnp.zeros_like(hidden)
    px[...] = jnp.zeros_like(px)

    def block(j, start, size, send, recv, device):
        part = buf.at[j, pl.ds(start, size)]
        return pltpu.make_async_remote_copy(
            src_ref=part, dst_ref=part, send_sem=send, recv_sem=recv,
            device_id={"tensor": device})

    def up(j, o, yy):
        return block(j, row(c, yy, o), rows, up_sem.at[j], zr_sem.at[j, o], index(z + 1, y, c))

    def down(j, o, yy):
        return block(j, row(c, yy, o), rows, dn_sem.at[j], zr_sem.at[j, o], index(z - 1, y, c))

    def across(j, o):
        return block(j, row(c, y, o), rows, ys_sem.at[j], yr_sem.at[j], index(z, 1 - y, c))

    def twin(j, which, yy):
        return block(
            j, row(c, yy, 0), rows * lines, cs_sem.at[j, which], cr_sem.at[j, which],
            index(z, y, 1 - c))

    def arrived(j, start, size, sem):
        part = buf.at[j, pl.ds(start, size)]
        pltpu.make_async_copy(part, part, sem).wait()

    def inside(j):
        return jnp.logical_and(j >= 0, j < jobs)

    def across_first(j):
        return lax.rem(j, 5) == 2

    def both(a, b):
        return jnp.logical_and(a, b)

    def line_first(j):
        return both(inside(j), jnp.logical_not(across_first(j)))

    def pair_ready(j):
        return both(inside(j), across_first(j))

    def relay(j, o, ups, downs, sides):
        if ups:
            @pl.when(z < lines - 1)
            def _():
                for yy in sides:
                    up(j, o, yy).start()
        if downs:
            @pl.when(z > 0)
            def _():
                for yy in sides:
                    down(j, o, yy).start()

    def step(s, carry):
        @pl.when(s < jobs)
        def _():
            arrived(s, row(c, y, z), rows, own_sem.at[s])
            across(s, z).start()

        @pl.when(line_first(s))
        def _():
            relay(s, z, True, True, (y,))

        p = s - SIDE

        @pl.when(pair_ready(p))
        def _():
            arrived(p, row(c, 1 - y, z), rows, yr_sem.at[p])
            relay(p, z, True, True, (y, 1 - y))

        for h in range(1, lines):
            j = s - h * HOP
            p = s - SIDE - h * HOP

            for o, there, ups in ((z - h, z >= h, True), (z + h, z + h < lines, False)):
                @pl.when(both(line_first(j), there))
                def _(o=o, ups=ups, j=j):
                    arrived(j, row(c, y, o), rows, zr_sem.at[j, o])
                    relay(j, o, ups, not ups, (y,))
                    across(j, o).start()

                @pl.when(both(pair_ready(p), there))
                def _(o=o, ups=ups, p=p):
                    arrived(p, 0, rows * 2, zr_sem.at[p, o])
                    relay(p, o, ups, not ups, (y, 1 - y))

        j1 = s - (lines - 1) * HOP

        @pl.when(line_first(j1))
        def _():
            twin(j1, 0, y).start()

        j2 = j1 - SIDE

        @pl.when(line_first(j2))
        def _():
            arrived(j2, row(c, 1 - y, 0), rows * lines, yr_sem.at[j2])
            twin(j2, 1, 1 - y).start()

        @pl.when(pair_ready(j2))
        def _():
            twin(j2, 0, y).start()
            twin(j2, 1, 1 - y).start()

        j3 = j2 - TWIN

        @pl.when(inside(j3))
        def _():
            arrived(j3, row(1 - c, y, 0), rows * lines, cr_sem.at[j3, 0])
            arrived(j3, row(1 - c, 1 - y, 0), rows * lines, cr_sem.at[j3, 1])

        @pl.when(jnp.logical_and(j3 >= 0, j3 < half))
        def _():
            wg_copy(j3).wait()

            @pl.when(j3 == 0)
            def _():
                small[0].wait()

            @pl.loop(0, gate.shape[0])
            def _(t):
                gate[t] += jnp.dot(
                    buf[j3], wgv[j3, :, pl.ds(pl.multiple_of(t * gate.shape[2], 128), gate.shape[2])],
                    preferred_element_type=F32)

            px[...] += nt(buf[j3], pinv[:, pl.ds(pl.multiple_of(j3 * CHUNK, CHUNK), CHUNK)])

        @pl.when(jnp.logical_and(j3 >= half, j3 < jobs))
        def _():
            k = j3 - half
            wd_copy(k).wait()

            @pl.loop(0, hidden.shape[0])
            def _(t):
                hidden[t] += nt(
                    buf[j3], wdv[k, pl.ds(pl.multiple_of(t * gate.shape[2], 128), hidden.shape[2])])

            @pl.when(k == 0)
            def _():
                @pl.loop(0, gate.shape[0])
                def _(t):
                    g = gate[t]
                    gate[t] = g / (1.0 + jnp.exp(-g))

                weighted()

        return carry

    width = px.shape[1]
    each = fpart.shape[0] // n
    per = each // examples

    def weighted():
        r = lax.broadcasted_iota(jnp.int32, (fpart.shape[0], width), 0)
        col = lax.broadcasted_iota(jnp.int32, (fpart.shape[0], width), 1)
        pick = jnp.where(r // examples == col, 1.0, 0.0).astype(F32)
        spread = nt(pick, px[...], lax.Precision.HIGHEST)
        e = lax.rem(lax.broadcasted_iota(jnp.int32, spread.shape, 0), examples)
        at = lax.broadcasted_iota(jnp.int32, spread.shape, 1)
        piece = at // rows
        oz = lax.rem(piece, lines)
        oy = lax.rem(piece // lines, 2)
        oc = piece // (2 * lines)
        token = index(oz, oy, oc) * rows + lax.rem(at, rows)
        begin = jnp.int32(0)
        mask = jnp.zeros(spread.shape, F32)
        for i in range(examples):
            end = begin + lens[i]
            mine = (e == i) & (token >= begin) & (token < end)
            mask = mask + jnp.where(mine, 1.0, 0.0)
            begin = end
        wt[...] = spread * mask

    lax.fori_loop(0, jobs + (lines - 1) * HOP + SIDE + TWIN, step, 0)

    small[1].wait()
    part_g = jnp.zeros((total, width), F32)
    for t in range(gate.shape[0]):
        grad_up = (hidden[t] * gate[t]).astype(BF16)
        part_g += nt(grad_up, poutv[:, t * gate.shape[2]:(t + 1) * gate.shape[2]])
    fpart[...] = jnp.dot(
        wt[...], part_g, precision=lax.Precision.HIGHEST, preferred_element_type=F32)

    def deal(i):
        d = lax.rem(me + i, n)
        return pltpu.make_async_remote_copy(
            src_ref=fpart.at[pl.ds(pl.multiple_of(d * each, each), each)],
            dst_ref=frecv.at[i - 1], send_sem=fs_sem.at[i - 1], recv_sem=fr_sem.at[i - 1],
            device_id={"tensor": d})

    for i in range(1, n):
        deal(i).start()
    small[2].wait()
    mine = fpart[pl.ds(pl.multiple_of(me * each, each), each)]
    for i in range(1, n):
        deal(i).wait_recv()
    for i in range(1, n):
        mine = mine + frecv[i - 1]
    for i in range(per):
        feats_ref[:, i * width:(i + 1) * width] = mine[i * examples:(i + 1) * examples]
    spart[0] = nt(feats_ref[...], qv[...], lax.Precision.HIGHEST)

    def tell(i):
        return pltpu.make_async_remote_copy(
            src_ref=spart.at[0], dst_ref=srecv.at[i - 1], send_sem=ss_sem.at[i - 1],
            recv_sem=sr_sem.at[i - 1], device_id={"tensor": lax.rem(me + i, n)})

    for i in range(1, n):
        tell(i).start()
    acc = spart[0]

    @pl.loop(0, jobs)
    def _(j):
        for width_of, test in ((1, line_first), (2, pair_ready)):
            @pl.when(test(j))
            def _(width_of=width_of):
                for zz in range(lines):
                    if zz < lines - 1:
                        @pl.when(z == zz)
                        def _(zz=zz):
                            arrived(j, 0, rows * (zz + 1) * width_of, up_sem.at[j])
                    if zz > 0:
                        @pl.when(z == zz)
                        def _(zz=zz):
                            arrived(j, 0, rows * (lines - zz) * width_of, dn_sem.at[j])

                arrived(j, 0, rows * (lines if width_of == 1 else 1), ys_sem.at[j])

        arrived(j, 0, rows * lines, cs_sem.at[j, 0])
        arrived(j, 0, rows * lines, cs_sem.at[j, 1])

    for i in range(1, n):
        deal(i).wait_send()
    for i in range(1, n):
        tell(i).wait_recv()
        acc = acc + srecv[i - 1]
    for i in range(1, n):
        tell(i).wait_send()
    scores_ref[...] = acc


def on_device(n, tokens, out_grad, gate_weight, down_weight, proj_in, proj_out, lengths, queries):
    rows, depth = tokens.shape
    hidden = gate_weight.shape[1]
    width = proj_in.shape[1]
    count, columns = queries.shape
    examples = lengths.shape[0]
    total = rows * n
    half = depth // CHUNK
    jobs = 2 * half
    tile = TILE if hidden % TILE == 0 else 128
    tiles = hidden // tile
    lines = n // 4
    dma = pltpu.SemaphoreType.DMA
    anywhere = pl.BlockSpec(memory_space=pl.ANY)
    vmem = pl.BlockSpec(memory_space=pltpu.VMEM)
    smem = pl.BlockSpec(memory_space=pltpu.SMEM)
    feat_rows = examples * width
    return pl.pallas_call(
        functools.partial(kernel, n),
        out_shape=(
            jax.ShapeDtypeStruct((examples, columns), F32),
            jax.ShapeDtypeStruct((examples, count), F32),
        ),
        in_specs=[anywhere] * 6 + [smem, anywhere],
        out_specs=(vmem, vmem),
        scratch_shapes=[
            pltpu.VMEM((jobs, total, CHUNK), BF16),
            pltpu.VMEM((half, CHUNK, hidden), BF16),
            pltpu.VMEM((half, hidden, CHUNK), BF16),
            pltpu.VMEM((tiles, total, tile), F32),
            pltpu.VMEM((tiles, total, tile), F32),
            pltpu.VMEM((width, depth), BF16),
            pltpu.VMEM((width, hidden), BF16),
            pltpu.VMEM((count, columns), F32),
            pltpu.VMEM((total, width), F32),
            pltpu.VMEM((feat_rows, total), F32),
            pltpu.VMEM((feat_rows, width), F32),
            pltpu.VMEM((n - 1, feat_rows // n, width), F32),
            pltpu.VMEM((2, examples, count), F32),
            pltpu.VMEM((n - 1, examples, count), F32),
            pltpu.VMEM((lines - 1, examples, count), F32),
            dma((jobs,)), dma((half,)), dma((half,)), dma((3,)),
            dma((jobs,)), dma((jobs,)), dma((jobs,)), dma((jobs, 2)),
            dma((jobs, lines)), dma((jobs,)), dma((jobs, 2)),
            dma((n - 1,)), dma((n - 1,)), dma((n - 1,)), dma((n - 1,)),
            dma((lines - 1,)), dma((lines - 1,)),
        ],
        compiler_params=pltpu.CompilerParams(
            collective_id=0, has_side_effects=True, vmem_limit_bytes=62 * 1024 * 1024
        ),
    )(tokens, out_grad, gate_weight, down_weight, proj_in.T, proj_out.T, lengths, queries)


def solution(mesh):
    placed = (
        P(("parts", "tensor"), None),
        P(("parts", "tensor"), None),
        P(None, "tensor"),
        P("tensor", None),
        P(),
        P("tensor", None),
        P("parts"),
        P(None, "tensor"),
    )
    return jax.shard_map(
        functools.partial(on_device, mesh.shape["tensor"]),
        mesh=mesh,
        in_specs=placed,
        out_specs=(P("parts", "tensor"), P("parts", None)),
        check_vma=False,
    )
```

```python
import functools

import jax
import jax.numpy as jnp
from jax import lax
from jax.experimental import pallas as pl
from jax.experimental.pallas import tpu as pltpu
from jax.sharding import PartitionSpec as P

F32 = jnp.float32
BF16 = jnp.bfloat16
CHUNK = 1024
HOP, SIDE, TWIN = 2, 2, 1
TILE = 1280


def nt(a, b, precision=None):
    return lax.dot_general(
        a, b, (((1,), (1,)), ((), ())), precision=precision, preferred_element_type=F32
    )


def kernel(
    n, tok, dy, wg, wd, pin, pout, lens, q, feats_ref, scores_ref,
    buf, wgv, wdv, gate, hidden, pinv, poutv, qv, px, wt, fpart, frecv, spart, srecv, zrecv,
    own_sem, wg_sem, wd_sem, misc_sem, up_sem, dn_sem, ys_sem, cs_sem, zr_sem, yr_sem, cr_sem,
    fs_sem, fr_sem, ss_sem, sr_sem, zs_sem, zrr_sem,
):
    me = lax.axis_index("tensor")
    rows = tok.shape[0]
    lines = n // 4
    c = lax.rem(me, 2)
    y = lax.rem(me // 2, 2)
    z = me // 4
    jobs = buf.shape[0]
    half = jobs // 2
    total = buf.shape[1]
    examples = lens.shape[0]

    def index(zz, yy, cc):
        return (zz * 2 + yy) * 2 + cc

    def row(cc, yy, zz):
        return pl.multiple_of(((cc * 2 + yy) * lines + zz) * rows, rows)

    barrier = pltpu.get_barrier_semaphore()
    for i in range(1, n):
        pl.semaphore_signal(barrier, inc=1, device_id={"tensor": lax.rem(me + i, n)})

    def own_copy(src, k, j):
        return pltpu.make_async_copy(
            src.at[:, pl.ds(pl.multiple_of(k * CHUNK, CHUNK), CHUNK)],
            buf.at[j, pl.ds(row(c, y, z), rows)], own_sem.at[j])

    def wg_copy(k):
        return pltpu.make_async_copy(
            wg.at[pl.ds(pl.multiple_of(k * CHUNK, CHUNK), CHUNK)], wgv.at[k], wg_sem.at[k])

    def wd_copy(k):
        return pltpu.make_async_copy(
            wd.at[:, pl.ds(pl.multiple_of(k * CHUNK, CHUNK), CHUNK)], wdv.at[k], wd_sem.at[k])

    small = [
        pltpu.make_async_copy(pin, pinv, misc_sem.at[0]),
        pltpu.make_async_copy(pout, poutv, misc_sem.at[1]),
        pltpu.make_async_copy(q, qv, misc_sem.at[2]),
    ]

    @pl.loop(0, half)
    def _(k):
        own_copy(tok, k, k).start()
        own_copy(dy, k, k + half).start()

    small[0].start()

    @pl.loop(0, half)
    def _(k):
        wg_copy(k).start()

    @pl.loop(0, half)
    def _(k):
        wd_copy(k).start()

    small[1].start()
    small[2].start()

    gate[...] = jnp.zeros_like(gate)
    hidden[...] = jnp.zeros_like(hidden)
    px[...] = jnp.zeros_like(px)

    pl.semaphore_wait(barrier, n - 1)

    def block(j, start, size, send, recv, device):
        part = buf.at[j, pl.ds(start, size)]
        return pltpu.make_async_remote_copy(
            src_ref=part, dst_ref=part, send_sem=send, recv_sem=recv,
            device_id={"tensor": device})

    def up(j, o, yy):
        return block(j, row(c, yy, o), rows, up_sem.at[j], zr_sem.at[j, o], index(z + 1, y, c))

    def down(j, o, yy):
        return block(j, row(c, yy, o), rows, dn_sem.at[j], zr_sem.at[j, o], index(z - 1, y, c))

    def across(j, o):
        return block(j, row(c, y, o), rows, ys_sem.at[j], yr_sem.at[j], index(z, 1 - y, c))

    def twin(j, which, yy):
        return block(
            j, row(c, yy, 0), rows * lines, cs_sem.at[j, which], cr_sem.at[j, which],
            index(z, y, 1 - c))

    def arrived(j, start, size, sem):
        part = buf.at[j, pl.ds(start, size)]
        pltpu.make_async_copy(part, part, sem).wait()

    def inside(j):
        return jnp.logical_and(j >= 0, j < jobs)

    def across_first(j):
        return lax.rem(j, 5) == 2

    def both(a, b):
        return jnp.logical_and(a, b)

    def line_first(j):
        return both(inside(j), jnp.logical_not(across_first(j)))

    def pair_ready(j):
        return both(inside(j), across_first(j))

    def relay(j, o, ups, downs, sides):
        if ups:
            @pl.when(z < lines - 1)
            def _():
                for yy in sides:
                    up(j, o, yy).start()
        if downs:
            @pl.when(z > 0)
            def _():
                for yy in sides:
                    down(j, o, yy).start()

    def step(s, carry):
        @pl.when(s < jobs)
        def _():
            arrived(s, row(c, y, z), rows, own_sem.at[s])
            across(s, z).start()

        @pl.when(line_first(s))
        def _():
            relay(s, z, True, True, (y,))

        p = s - SIDE

        @pl.when(pair_ready(p))
        def _():
            arrived(p, row(c, 1 - y, z), rows, yr_sem.at[p])
            relay(p, z, True, True, (y, 1 - y))

        for h in range(1, lines):
            j = s - h * HOP
            p = s - SIDE - h * HOP

            for o, there, ups in ((z - h, z >= h, True), (z + h, z + h < lines, False)):
                @pl.when(both(line_first(j), there))
                def _(o=o, ups=ups, j=j):
                    arrived(j, row(c, y, o), rows, zr_sem.at[j, o])
                    relay(j, o, ups, not ups, (y,))
                    across(j, o).start()

                @pl.when(both(pair_ready(p), there))
                def _(o=o, ups=ups, p=p):
                    arrived(p, 0, rows * 2, zr_sem.at[p, o])
                    relay(p, o, ups, not ups, (y, 1 - y))

        j1 = s - (lines - 1) * HOP

        @pl.when(line_first(j1))
        def _():
            twin(j1, 0, y).start()

        j2 = j1 - SIDE

        @pl.when(line_first(j2))
        def _():
            arrived(j2, row(c, 1 - y, 0), rows * lines, yr_sem.at[j2])
            twin(j2, 1, 1 - y).start()

        @pl.when(pair_ready(j2))
        def _():
            twin(j2, 0, y).start()
            twin(j2, 1, 1 - y).start()

        j3 = j2 - TWIN

        @pl.when(inside(j3))
        def _():
            arrived(j3, row(1 - c, y, 0), rows * lines, cr_sem.at[j3, 0])
            arrived(j3, row(1 - c, 1 - y, 0), rows * lines, cr_sem.at[j3, 1])

        @pl.when(jnp.logical_and(j3 >= 0, j3 < half))
        def _():
            wg_copy(j3).wait()

            @pl.when(j3 == 0)
            def _():
                small[0].wait()

            @pl.loop(0, gate.shape[0])
            def _(t):
                gate[t] += jnp.dot(
                    buf[j3], wgv[j3, :, pl.ds(pl.multiple_of(t * gate.shape[2], 128), gate.shape[2])],
                    preferred_element_type=F32)

            px[...] += nt(buf[j3], pinv[:, pl.ds(pl.multiple_of(j3 * CHUNK, CHUNK), CHUNK)])

        @pl.when(jnp.logical_and(j3 >= half, j3 < jobs))
        def _():
            k = j3 - half
            wd_copy(k).wait()

            @pl.loop(0, hidden.shape[0])
            def _(t):
                hidden[t] += nt(
                    buf[j3], wdv[k, pl.ds(pl.multiple_of(t * gate.shape[2], 128), hidden.shape[2])])

            @pl.when(k == 0)
            def _():
                @pl.loop(0, gate.shape[0])
                def _(t):
                    g = gate[t]
                    gate[t] = g / (1.0 + jnp.exp(-g))

                weighted()

        return carry

    width = px.shape[1]
    each = fpart.shape[0] // n
    per = each // examples

    def weighted():
        r = lax.broadcasted_iota(jnp.int32, (fpart.shape[0], width), 0)
        col = lax.broadcasted_iota(jnp.int32, (fpart.shape[0], width), 1)
        pick = jnp.where(r // examples == col, 1.0, 0.0).astype(F32)
        spread = nt(pick, px[...], lax.Precision.HIGHEST)
        e = lax.rem(lax.broadcasted_iota(jnp.int32, spread.shape, 0), examples)
        at = lax.broadcasted_iota(jnp.int32, spread.shape, 1)
        piece = at // rows
        oz = lax.rem(piece, lines)
        oy = lax.rem(piece // lines, 2)
        oc = piece // (2 * lines)
        token = index(oz, oy, oc) * rows + lax.rem(at, rows)
        begin = jnp.int32(0)
        mask = jnp.zeros(spread.shape, F32)
        for i in range(examples):
            end = begin + lens[i]
            mine = (e == i) & (token >= begin) & (token < end)
            mask = mask + jnp.where(mine, 1.0, 0.0)
            begin = end
        wt[...] = spread * mask

    lax.fori_loop(0, jobs + (lines - 1) * HOP + SIDE + TWIN, step, 0)

    small[1].wait()
    part_g = jnp.zeros((total, width), F32)
    for t in range(gate.shape[0]):
        grad_up = (hidden[t] * gate[t]).astype(BF16)
        part_g += nt(grad_up, poutv[:, t * gate.shape[2]:(t + 1) * gate.shape[2]])
    fpart[...] = jnp.dot(
        wt[...], part_g, precision=lax.Precision.HIGHEST, preferred_element_type=F32)

    def deal(i):
        d = lax.rem(me + i, n)
        return pltpu.make_async_remote_copy(
            src_ref=fpart.at[pl.ds(pl.multiple_of(d * each, each), each)],
            dst_ref=frecv.at[i - 1], send_sem=fs_sem.at[i - 1], recv_sem=fr_sem.at[i - 1],
            device_id={"tensor": d})

    for i in range(1, n):
        deal(i).start()
    small[2].wait()
    mine = fpart[pl.ds(pl.multiple_of(me * each, each), each)]
    for i in range(1, n):
        deal(i).wait_recv()
    for i in range(1, n):
        mine = mine + frecv[i - 1]
    for i in range(per):
        feats_ref[:, i * width:(i + 1) * width] = mine[i * examples:(i + 1) * examples]
    spart[0] = nt(feats_ref[...], qv[...], lax.Precision.HIGHEST)

    def tell(i):
        return pltpu.make_async_remote_copy(
            src_ref=spart.at[0], dst_ref=srecv.at[i - 1], send_sem=ss_sem.at[i - 1],
            recv_sem=sr_sem.at[i - 1], device_id={"tensor": lax.rem(me + i, n)})

    for i in range(1, n):
        tell(i).start()
    acc = spart[0]

    @pl.loop(0, jobs)
    def _(j):
        for width_of, test in ((1, line_first), (2, pair_ready)):
            @pl.when(test(j))
            def _(width_of=width_of):
                for zz in range(lines):
                    if zz < lines - 1:
                        @pl.when(z == zz)
                        def _(zz=zz):
                            arrived(j, 0, rows * (zz + 1) * width_of, up_sem.at[j])
                    if zz > 0:
                        @pl.when(z == zz)
                        def _(zz=zz):
                            arrived(j, 0, rows * (lines - zz) * width_of, dn_sem.at[j])

                arrived(j, 0, rows * (lines if width_of == 1 else 1), ys_sem.at[j])

        arrived(j, 0, rows * lines, cs_sem.at[j, 0])
        arrived(j, 0, rows * lines, cs_sem.at[j, 1])

    for i in range(1, n):
        deal(i).wait_send()
    for i in range(1, n):
        tell(i).wait_recv()
        acc = acc + srecv[i - 1]
    for i in range(1, n):
        tell(i).wait_send()
    scores_ref[...] = acc


def on_device(n, tokens, out_grad, gate_weight, down_weight, proj_in, proj_out, lengths, queries):
    rows, depth = tokens.shape
    hidden = gate_weight.shape[1]
    width = proj_in.shape[1]
    count, columns = queries.shape
    examples = lengths.shape[0]
    total = rows * n
    half = depth // CHUNK
    jobs = 2 * half
    tile = TILE if hidden % TILE == 0 else 128
    tiles = hidden // tile
    lines = n // 4
    dma = pltpu.SemaphoreType.DMA
    anywhere = pl.BlockSpec(memory_space=pl.ANY)
    vmem = pl.BlockSpec(memory_space=pltpu.VMEM)
    smem = pl.BlockSpec(memory_space=pltpu.SMEM)
    feat_rows = examples * width
    return pl.pallas_call(
        functools.partial(kernel, n),
        out_shape=(
            jax.ShapeDtypeStruct((examples, columns), F32),
            jax.ShapeDtypeStruct((examples, count), F32),
        ),
        in_specs=[anywhere] * 6 + [smem, anywhere],
        out_specs=(vmem, vmem),
        scratch_shapes=[
            pltpu.VMEM((jobs, total, CHUNK), BF16),
            pltpu.VMEM((half, CHUNK, hidden), BF16),
            pltpu.VMEM((half, hidden, CHUNK), BF16),
            pltpu.VMEM((tiles, total, tile), F32),
            pltpu.VMEM((tiles, total, tile), F32),
            pltpu.VMEM((width, depth), BF16),
            pltpu.VMEM((width, hidden), BF16),
            pltpu.VMEM((count, columns), F32),
            pltpu.VMEM((total, width), F32),
            pltpu.VMEM((feat_rows, total), F32),
            pltpu.VMEM((feat_rows, width), F32),
            pltpu.VMEM((n - 1, feat_rows // n, width), F32),
            pltpu.VMEM((2, examples, count), F32),
            pltpu.VMEM((n - 1, examples, count), F32),
            pltpu.VMEM((lines - 1, examples, count), F32),
            dma((jobs,)), dma((half,)), dma((half,)), dma((3,)),
            dma((jobs,)), dma((jobs,)), dma((jobs,)), dma((jobs, 2)),
            dma((jobs, lines)), dma((jobs,)), dma((jobs, 2)),
            dma((n - 1,)), dma((n - 1,)), dma((n - 1,)), dma((n - 1,)),
            dma((lines - 1,)), dma((lines - 1,)),
        ],
        compiler_params=pltpu.CompilerParams(
            collective_id=0, has_side_effects=True, vmem_limit_bytes=62 * 1024 * 1024
        ),
    )(tokens, out_grad, gate_weight, down_weight, proj_in.T, proj_out.T, lengths, queries)


def solution(mesh):
    placed = (
        P(("parts", "tensor"), None),
        P(("parts", "tensor"), None),
        P(None, "tensor"),
        P("tensor", None),
        P(),
        P("tensor", None),
        P("parts"),
        P(None, "tensor"),
    )
    return jax.shard_map(
        functools.partial(on_device, mesh.shape["tensor"]),
        mesh=mesh,
        in_specs=placed,
        out_specs=(P("parts", "tensor"), P("parts", None)),
        check_vma=False,
    )
```
